1024 devices in a mesh: grp: 64 (over x_hi, z, core), exp: 16 (over y, x_lo).
Axes of the slice: x: 8 (x_hi: 4, x_lo: 2; x = x_hi * 2 + x_lo), y: 8, z: 8, core: 2. Of those that a mesh axis runs over, the one named last changes fastest.
Arguments:
- hidden: bfloat16 [64, 64, 7168], P('grp', 'exp'), may hold values from -6 to 6
- norm_gain: float32 [7168], replicated, may hold values from 0.1 to 1.9
- route: int32 [64, 64, 1], P('grp', 'exp'), may hold values from 0 to 1; in each aligned block of 4 rows (0 to 3, 4 to 7, ..., all dimensions but the last counted through in order) at most 3 rows name the same one
- route_weight: float32 [64, 64], P('grp', 'exp'), may hold values from 0.2 to 1
- resident: bfloat16 [2, 2048, 7168], P(None, 'exp'), may hold values from -0.0625 to 0.0625
- sectioned: bfloat16 [64, 512, 7168], P('grp', 'exp'), may hold values from -0.1875 to 0.1875
- owner: int32 [64], replicated, may hold values from 0 to 63, each once
Outputs:
- moe_out: bfloat16 [64, 64, 7168], P('grp', 'exp')
The draws below stay inside these ranges and needn't reach their ends.
Inputs may be any that keep to these rules, and one draw needn't show every extreme that they name: `route`: each row names one of the 2 experts. Among the 4 rows of one device at most 3 name the same expert, and in every draw some device has exactly 3 rows naming one expert. Every group number appears exactly once, so the 4 buckets have distinct owner groups.
All inputs are finite; a program needn't handle non-finite values.
Results may differ from the reference program's by a relative error of at most 0.0071.
Values may be sent and summed in bfloat16 or wider, within the bound.
A program may use at most 32 MiB of HBM per device.

```python
import math
import jax
import jax.numpy as jnp
import numpy as np
from jax import lax

D = 7168
FF_WIN = 1024
E_WIN = 2
BUCKETS = 4
ROWS_DEV = 4
CAP = 3
ROWS = 64
UNITS = 512
FB = 32
N_GRP = 64
N_EXP = 16


def shard_levels(own_key, shape, pieces, smallest, largest):
    loudness, own = 1.0, jax.random.fold_in(own_key, 6)
    for position, parts in pieces:
        steps = jnp.exp(jax.random.uniform(jax.random.fold_in(own, position), (parts,), jnp.float32, smallest / len(pieces), largest / len(pieces)))
        loudness = loudness * jnp.repeat(steps, shape[position] // parts).reshape([-1 if axis == position else 1 for axis in range(len(shape))])
    return loudness


def shared_out(stream_key, own, number, rows, amount, top, bound, skew):
    sequence = jax.random.permutation(stream_key, amount)
    packed, ordinary = shares(amount, rows * top, bound, skew, True), shares(amount, rows * top, bound, skew, False)
    places = jnp.arange(amount)

    def named(lengths, rotation):
        used = int((lengths > 0).sum())
        fixed = max(1, used // 4)
        passed = fixed + (places - fixed + rotation * (used - fixed)) % max(1, amount - fixed)
        return jnp.zeros((amount,), jnp.int32).at[sequence[jnp.where(places < fixed, places, passed)]].set(jnp.asarray(lengths, jnp.int32))

    lengths = jnp.where(number % 4 == 0, named(packed, number // 4), named(ordinary, number - number // 4 - 1))
    mixed = jax.random.permutation(jax.random.fold_in(own, 3), amount)
    source_of, sink = mixed[0:amount // 2 * 2:2], mixed[1:amount // 2 * 2:2]
    margin = jnp.minimum(lengths[source_of] - 1, bound - lengths[sink]) // 2
    margin = jnp.where((source_of == sequence[0]) | (sink == sequence[0]) | (lengths[sink] == 0), 0, jnp.maximum(margin, 0))
    passed = jax.random.randint(jax.random.fold_in(own, 4), (amount // 2,), 0, 1 << 20) % (margin + 1)
    lengths = lengths.at[source_of].add(-passed).at[sink].add(passed)
    members = jnp.searchsorted(jnp.cumsum(lengths), jnp.arange(rows * top), side="right").astype(jnp.int32)
    listing = members.reshape(top, rows).T
    listing = listing[jax.random.permutation(jax.random.fold_in(own, 1), rows)]
    rotation = jax.random.randint(jax.random.fold_in(own, 2), (rows, 1), 0, top)
    return jnp.take_along_axis(listing, (jnp.arange(top)[None, :] + rotation) % top, axis=1)


def shares(amount, total, bound, skew, full):
    loads = [(1 << 20) // math.isqrt(rank ** skew) + 1 for rank in range(1, amount + 1)]
    largest = bound if full else min(bound, max(-(-total // amount), total * loads[0] // sum(loads)))
    least = 1 if total - largest >= amount - 1 else 0
    counts, surplus = [largest] + [least] * (amount - 1), total - largest - least * (amount - 1)
    while surplus > 0:
        candidates = [i for i in range(1, amount) if counts[i] < largest] or [i for i in range(1, amount) if counts[i] < bound]
        whole, budget = sum([loads[i] for i in candidates]), surplus
        for i in candidates:
            extra = min(bound - counts[i], max(1, budget * loads[i] // whole), surplus)
            counts[i] = counts[i] + extra
            surplus = surplus - extra
    return np.array(counts)


def normal_values(key, dims, scale, bound, cuts=(), held_as=jnp.bfloat16):
    values = jax.random.normal(key, dims, jnp.float32) * scale
    if len(cuts) > 0:
        values = shard_levels(key, dims, cuts, -0.22, 0.18) * values
    return jnp.clip(values, min=-bound, max=bound).astype(held_as)


def setup_inputs(seed: int = 0) -> dict:
    streams_of = jax.random.split(jax.random.key(seed), 8)
    hidden = normal_values(streams_of[0], (N_GRP, ROWS, D), 1.0, 6.0, ((0, 64), (1, 16)))
    norm_gain = jnp.clip(1.0 + 0.18 * jax.random.normal(streams_of[1], (D,), jnp.float32), 0.1, 1.9)
    route_keys = jax.random.split(jax.random.fold_in(streams_of[2], 1), N_GRP * ROWS // ROWS_DEV)
    route_turns = jax.random.permutation(jax.random.fold_in(streams_of[2], 3), N_GRP * ROWS // ROWS_DEV)
    route = jax.vmap(lambda own, number: shared_out(jax.random.fold_in(streams_of[2], 2), own, number, ROWS_DEV, E_WIN, 1, CAP, 0))(route_keys, route_turns).reshape((N_GRP, ROWS, 1))
    route_weight = jnp.clip(0.2 + 0.8 * jax.random.uniform(streams_of[3], (N_GRP, ROWS), jnp.float32) ** shard_levels(streams_of[3], (N_GRP, ROWS), ((0, 64), (1, 16)), -0.2, 0.2), 0.2, 1.0)
    resident = normal_values(streams_of[4], (2, N_EXP * BUCKETS * FB, D), D ** -0.5, 0.0625, ((1, 16),))
    sectioned = normal_values(streams_of[5], (N_GRP, UNITS, D), FF_WIN ** -0.5, 0.1875, ((0, 64), (1, 16)))
    owner = jax.random.permutation(streams_of[6], N_GRP).astype(jnp.int32)
    return dict(hidden=hidden, norm_gain=norm_gain, route=route, route_weight=route_weight, resident=resident, sectioned=sectioned, owner=owner)


epsilon = 1e-06

def reference(hidden, norm_gain, route, route_weight, resident, sectioned, owner):
    live = sectioned[owner[:BUCKETS]]
    down_blocks = live.reshape(BUCKETS, N_EXP, FB, D)
    down_blocks = jnp.transpose(down_blocks, (1, 0, 2, 3)).reshape(N_EXP, BUCKETS * FB, D)
    gate_blocks = jnp.transpose(resident.reshape(2, N_EXP, BUCKETS * FB, D), (1, 0, 2, 3))
    row_data = hidden.reshape(-1, D).astype(jnp.float32)
    scale = lax.rsqrt(lax.optimization_barrier(jnp.mean(row_data * row_data, axis=1, keepdims=True)) + epsilon)
    normed = (row_data * scale * norm_gain[None, :]).astype(jnp.bfloat16)
    expert_ids = route.reshape(-1)
    shards = N_EXP // E_WIN

    def accumulate(running, inputs):
        gate_up, down_rows, device = inputs
        gate_part = lax.dot_general(normed, gate_up[0], (((1,), (1,)), ((), ())), preferred_element_type=jnp.float32)
        up_part = lax.dot_general(normed, gate_up[1], (((1,), (1,)), ((), ())), preferred_element_type=jnp.float32)
        activation = (jax.nn.silu(gate_part) * up_part).astype(jnp.bfloat16)
        partial_value = jnp.dot(activation, down_rows, preferred_element_type=jnp.float32).astype(jnp.bfloat16)
        partial_value = lax.optimization_barrier(partial_value).astype(jnp.float32)
        chosen = (expert_ids == device // shards)[:, None]
        return (running + jnp.where(chosen, partial_value, jnp.zeros_like(partial_value)), None)
    start = jnp.zeros((normed.shape[0], D), jnp.float32)
    running, _ = lax.scan(accumulate, start, (gate_blocks, down_blocks, jnp.arange(N_EXP, dtype=jnp.int32)))
    result = (running * route_weight.reshape(-1, 1)).astype(jnp.bfloat16)
    return result.reshape(N_GRP, -1, D)
```

```python
import jax
import jax.numpy as jnp
from jax import lax
from jax.experimental import pallas as pl
from jax.experimental.pallas import tpu as pltpu
from jax.sharding import PartitionSpec as P

MESH = pl.DeviceIdType.MESH
BUCKETS = 4
EPSILON = 1e-06
XH, Z, Y = 4, 8, 8
HALF = 4
ZW = 7
SUB = 16
COLS = 256
QUARTER = ZW * COLS
FLAG = 128


def kernel(
    owner, hidden, gain, route, weight, resident, sectioned,
    out,
    gate_up, staged, rows, perm, chunks, chosen, down, act, acts, product, sends, partials, sums, finals, gathered,
    local_sem, row_send, row_recv, a_send, a_recv, a_local, w_send, w_recv, w_local, act_send, act_recv, act_local,
    y_send, y_recv, y_local, z_send, z_recv, z_local,
):
    g, e = lax.axis_index("grp"), lax.axis_index("exp")
    xh, z, c = g // 16, (g // 2) % 8, g % 2
    y, xl = e // 2, e % 2
    half, quarter = y // HALF, y % HALF

    def wait_for(blocks, sem):
        pltpu.make_async_copy(chunks.at[pl.ds(0, blocks)], chunks.at[pl.ds(0, blocks)], sem).wait()

    def grp(a, b, d):
        return (a * Z + b) * 2 + d

    load = pltpu.make_async_copy(resident, gate_up, local_sem)
    load.start()

    barrier = pltpu.get_barrier_semaphore()

    def greet(gg, ee):
        pl.semaphore_signal(barrier, inc=1, device_id=(gg, ee), device_id_type=MESH)

    def greet_plane(i, carry):
        greet((g + i) % 64, e)
        return carry

    def greet_exp(i, carry):
        greet(g, (e + i) % 16)
        return carry

    def greet_acts(i, carry):
        greet(grp(xh, (z + 1 + i % 7) % Z, c), (half * HALF + (quarter + 1 + i // 7) % HALF) * 2 + xl)
        return carry

    def greet_down(i, carry):
        k = (xh * 2 + c + 1 + i % 7) % 8
        greet(grp(k // 2, z, k % 2), (half * HALF + (quarter + 1 + i // 7) % HALF) * 2 + xl)
        return carry

    lax.fori_loop(1, 64, greet_plane, 0)
    lax.fori_loop(1, 16, greet_exp, 0)
    lax.fori_loop(0, 21, greet_acts, 0)
    lax.fori_loop(0, 21, greet_down, 0)

    data = hidden[...].astype(jnp.float32)
    scale = lax.rsqrt(jnp.mean(data * data, axis=1, keepdims=True) + EPSILON)
    normed = data * scale * gain[...]
    flags = jnp.broadcast_to(route[...].astype(jnp.float32), (4, FLAG))
    for j in range(4):
        staged[4 * j : 4 * j + 4, 0:QUARTER] = normed[:, j * QUARTER : (j + 1) * QUARTER]
        staged[4 * j : 4 * j + 4, QUARTER:] = flags
    rows[e] = staged[...].astype(jnp.bfloat16)

    to = lax.broadcasted_iota(jnp.int32, (256, 256), 0)
    source = lax.broadcasted_iota(jnp.int32, (256, 256), 1)
    wanted = ((to % 64) // 4) * 16 + (to // 64) * 4 + to % 4
    perm[...] = jnp.where(wanted == source, 1.0, 0.0).astype(jnp.bfloat16)

    pl.semaphore_wait(barrier, 63 + 15 + 21 + 21)

    def slot(dy, other):
        return ((y + dy + 8) % 8) * 2 + (1 - xl if other else xl)

    def pass_on(s, ee):
        pltpu.make_async_remote_copy(
            src_ref=rows.at[s], dst_ref=rows.at[s], send_sem=row_send, recv_sem=row_recv.at[s],
            device_id=(g, ee), device_id_type=MESH,
        ).start()

    def row_wait(s):
        pltpu.make_async_copy(rows.at[s], rows.at[s], row_recv.at[s]).wait()

    right, left, across = slot(1, False), slot(-1, False), slot(0, True)
    pass_on(e, across)
    pass_on(e, right)
    pass_on(e, left)

    def a_dest(i):
        k = (xh * 2 + c + i // 8) % 8
        zz = (z + i % 8) % 8
        return k // 2, zz, k % 2

    def a_source(aa, zz, cc):
        column = pl.multiple_of(aa * QUARTER + zz * COLS, 128)
        return sectioned.at[pl.ds(pl.multiple_of(cc * SUB, SUB), SUB), pl.ds(column, COLS)]

    def a_start(i, carry):
        aa, zz, cc = a_dest(i)

        @pl.when(zz < ZW)
        def _():
            pltpu.make_async_remote_copy(
                src_ref=a_source(aa, zz, cc), dst_ref=chunks.at[g], send_sem=a_send, recv_sem=a_recv,
                device_id=(grp(aa, zz, cc), e), device_id_type=MESH,
            ).start()

        return carry

    @pl.when(z < ZW)
    def _():
        pltpu.make_async_copy(a_source(xh, z, c), chunks.at[g], a_local).start()

    lax.fori_loop(1, 64, a_start, 0)

    row_wait(across)
    pass_on(across, right)
    pass_on(across, left)
    for d in (1, 2, 3):
        for other in (False, True):
            s = slot(-d, other)
            row_wait(s)
            if d < 3 or not other:
                pass_on(s, right)
            s = slot(d, other)
            row_wait(s)
            if d < 3 or other:
                pass_on(s, left)
    row_wait(slot(4, False))
    row_wait(slot(4, True))

    load.wait()
    flat = rows[...].reshape(256, QUARTER + FLAG)
    ordered = jnp.dot(perm[...], flat, preferred_element_type=jnp.float32).astype(jnp.bfloat16)
    gates = jnp.zeros((64, 128), jnp.float32)
    ups = jnp.zeros((64, 128), jnp.float32)
    for j in range(4):
        part = ordered[j * 64 : (j + 1) * 64, 0:QUARTER]
        lanes = slice(j * QUARTER, (j + 1) * QUARTER)
        gates += lax.dot_general(
            part, gate_up[0, :, lanes], (((1,), (1,)), ((), ())), preferred_element_type=jnp.float32
        )
        ups += lax.dot_general(
            part, gate_up[1, :, lanes], (((1,), (1,)), ((), ())), preferred_element_type=jnp.float32
        )
    expert = ordered[0:64, QUARTER:].astype(jnp.float32)
    mine = jnp.abs(expert - half.astype(jnp.float32)) < 0.5
    act[...] = jnp.where(mine, jax.nn.silu(gates) * ups, 0.0).astype(jnp.bfloat16)

    def act_place():
        return acts.at[z, :, pl.ds(pl.multiple_of(quarter * 128, 128), 128)]

    def act_start(i, carry):
        zz = (z + i % 8) % 8
        ee = (half * HALF + (quarter + i // 8) % HALF) * 2 + xl

        @pl.when(zz < ZW)
        def _():
            pltpu.make_async_remote_copy(
                src_ref=act, dst_ref=act_place(), send_sem=act_send, recv_sem=act_recv,
                device_id=(grp(xh, zz, c), ee), device_id_type=MESH,
            ).start()

        return carry

    @pl.when(z < ZW)
    def _():
        pltpu.make_async_copy(act, act_place(), act_local).start()

    lax.fori_loop(1, 32, act_start, 0)

    @pl.when(z < ZW)
    def _():
        pltpu.make_async_copy(a_source(xh, z, c), chunks.at[g], a_local).wait()
        wait_for(63, a_recv)
        for b in range(BUCKETS):
            chosen[b] = chunks[owner[b]]

        yy = half * HALF + xh
        place = down.at[quarter, :, c]

        @pl.when(xh == quarter)
        def _():
            pltpu.make_async_copy(chosen, place, w_local).start()

        for i in range(8):
            k = (xh * 2 + c + i) % 8

            def w_start():
                pltpu.make_async_remote_copy(
                    src_ref=chosen, dst_ref=place, send_sem=w_send, recv_sem=w_recv,
                    device_id=(grp(k // 2, z, k % 2), yy * 2 + xl), device_id_type=MESH,
                ).start()

            if i == 0:
                pl.when(xh != quarter)(w_start)
            else:
                w_start()

        pltpu.make_async_copy(act, act_place(), act_local).wait()
        wait_for(62, act_recv)

        @pl.when(xh == quarter)
        def _():
            wait_for(28, w_recv)
            pltpu.make_async_copy(chosen, place, w_local).wait()

        @pl.when(xh != quarter)
        def _():
            wait_for(32, w_recv)

        product[...] = jnp.dot(
            acts[...].reshape(512, 512), down[...].reshape(512, COLS), preferred_element_type=jnp.float32
        )
        for ee in range(16):
            for zz in range(8):
                sends[ee * 32 + zz * 4 : ee * 32 + zz * 4 + 4, :] = product[zz * 64 + ee * 4 : zz * 64 + ee * 4 + 4, :]
        gathered[...] = sends[...].astype(jnp.bfloat16).reshape(16, 32, COLS)

        def y_start(i, carry):
            ee = (e + i) % 16
            pltpu.make_async_remote_copy(
                src_ref=gathered.at[ee], dst_ref=partials.at[e], send_sem=y_send, recv_sem=y_recv,
                device_id=(g, ee), device_id_type=MESH,
            ).start()
            return carry

        lax.fori_loop(1, 16, y_start, 0)
        own = pltpu.make_async_copy(gathered.at[e], partials.at[e], y_local)
        own.start()
        own.wait()
        wait_for(30, y_recv)
        for q in range(4):
            total = jnp.zeros((32, COLS), jnp.float32)
            for hh in range(2):
                for ll in range(2):
                    total += partials[(hh * HALF + q) * 2 + ll].astype(jnp.float32)
            product[q * 32 : q * 32 + 32, :] = total
        for q in range(4):
            for zz in range(8):
                sends[zz * 16 + q * 4 : zz * 16 + q * 4 + 4, :] = product[q * 32 + zz * 4 : q * 32 + zz * 4 + 4, :]
        sums[...] = sends[0:128, :].astype(jnp.bfloat16).reshape(8, 16, COLS)

        for i in range(1, 8):
            zz = (z + i) % 8
            pltpu.make_async_remote_copy(
                src_ref=sums.at[zz], dst_ref=finals.at[z], send_sem=z_send, recv_sem=z_recv,
                device_id=(grp(xh, zz, c), e), device_id_type=MESH,
            ).start()
        own_z = pltpu.make_async_copy(sums.at[z], finals.at[z], z_local)
        own_z.start()
        own_z.wait()

    @pl.when(z < ZW)
    def _():
        wait_for(6, z_recv)

    @pl.when(z == ZW)
    def _():
        wait_for(7, z_recv)

    scaled = weight[...]
    sends[0 : ZW * SUB, :] = finals[0:ZW].astype(jnp.float32).reshape(ZW * SUB, COLS)
    for zz in range(ZW):
        for q in range(4):
            lanes = slice(q * QUARTER + zz * COLS, q * QUARTER + (zz + 1) * COLS)
            out[:, lanes] = (sends[zz * 16 + q * 4 : zz * 16 + q * 4 + 4, :] * scaled).astype(jnp.bfloat16)

    pltpu.make_async_copy(rows.at[pl.ds(0, 15)], rows.at[pl.ds(0, 15)], row_send).wait()

    @pl.when(z == ZW)
    def _():
        wait_for(56, a_send)
        wait_for(56, act_send)

    @pl.when(z < ZW)
    def _():
        wait_for(55, a_send)
        wait_for(54, act_send)
        wait_for(30, y_send)
        wait_for(7, z_send)

        @pl.when(xh == quarter)
        def _():
            wait_for(28, w_send)

        @pl.when(xh != quarter)
        def _():
            wait_for(32, w_send)


def per_device(hidden, norm_gain, route, route_weight, resident, sectioned, owner):
    width = hidden.shape[-1]
    vmem, anywhere = pl.BlockSpec(memory_space=pltpu.VMEM), pl.BlockSpec(memory_space=pl.ANY)
    half = lambda *shape: pltpu.VMEM(shape, jnp.bfloat16)
    single = lambda *shape: pltpu.VMEM(shape, jnp.float32)
    dma = pltpu.SemaphoreType.DMA
    result = pl.pallas_call(
        kernel,
        out_shape=jax.ShapeDtypeStruct((4, width), jnp.bfloat16),
        in_specs=[pl.BlockSpec(memory_space=pltpu.SMEM), vmem, vmem, vmem, vmem, anywhere, anywhere],
        out_specs=vmem,
        scratch_shapes=[
            half(2, 128, width),
            single(SUB, QUARTER + FLAG),
            half(16, SUB, QUARTER + FLAG),
            half(256, 256),
            half(64, SUB, COLS),
            half(BUCKETS, SUB, COLS),
            half(4, BUCKETS, 2, SUB, COLS),
            half(64, 128),
            half(8, 64, 512),
            single(512, COLS),
            single(512, COLS),
            half(16, 32, COLS),
            half(8, SUB, COLS),
            half(8, SUB, COLS),
            half(16, 32, COLS),
            dma, dma, dma((16,)), dma, dma, dma, dma, dma, dma, dma, dma, dma, dma, dma, dma, dma, dma, dma,
        ],
        compiler_params=pltpu.CompilerParams(
            collective_id=0, has_side_effects=True, vmem_limit_bytes=40 * 2**20
        ),
    )(
        owner,
        hidden[0],
        norm_gain[None, :],
        route[0],
        route_weight.reshape(4, 1),
        resident,
        sectioned[0],
    )
    return result[None]


def solution(mesh):
    in_specs = (
        P("grp", "exp", None),
        P(),
        P("grp", "exp", None),
        P("grp", "exp"),
        P(None, "exp", None),
        P("grp", "exp", None),
        P(),
    )
    return jax.shard_map(
        per_device, mesh=mesh, in_specs=in_specs, out_specs=P("grp", "exp", None), check_vma=False
    )
```

```python
import jax
import jax.numpy as jnp
from jax import lax
from jax.experimental import pallas as pl
from jax.experimental.pallas import tpu as pltpu
from jax.sharding import PartitionSpec as P

MESH = pl.DeviceIdType.MESH
BUCKETS = 4
EPSILON = 1e-06
XH, Z, Y = 4, 8, 8
HALF = 4
ZW = 7
SUB = 16
COLS = 256
QUARTER = ZW * COLS
FLAG = 128


def kernel(
    owner, hidden, gain, route, weight, resident, sectioned,
    out,
    gate_up, staged, rows, perm, chunks, chosen, down, act, acts, product, sends, partials, sums, finals, gathered,
    local_sem, row_send, row_recv, a_send, a_recv, a_local, w_send, w_recv, w_local, act_send, act_recv, act_local,
    y_send, y_recv, y_local, z_send, z_recv, z_local,
):
    g, e = lax.axis_index("grp"), lax.axis_index("exp")
    xh, z, c = g // 16, (g // 2) % 8, g % 2
    y, xl = e // 2, e % 2
    half, quarter = y // HALF, y % HALF

    def wait_for(blocks, sem):
        pltpu.make_async_copy(chunks.at[pl.ds(0, blocks)], chunks.at[pl.ds(0, blocks)], sem).wait()

    def grp(a, b, d):
        return (a * Z + b) * 2 + d

    load = pltpu.make_async_copy(resident, gate_up, local_sem)
    load.start()

    barrier = pltpu.get_barrier_semaphore()

    def greet(gg, ee):
        pl.semaphore_signal(barrier, inc=1, device_id=(gg, ee), device_id_type=MESH)

    def greet_plane(i, carry):
        greet((g + i) % 64, e)
        return carry

    def greet_exp(i, carry):
        greet(g, (e + i) % 16)
        return carry

    def greet_acts(i, carry):
        greet(grp(xh, (z + 1 + i % 7) % Z, c), (half * HALF + (quarter + 1 + i // 7) % HALF) * 2 + xl)
        return carry

    def greet_down(i, carry):
        k = (xh * 2 + c + 1 + i % 7) % 8
        greet(grp(k // 2, z, k % 2), (half * HALF + (quarter + 1 + i // 7) % HALF) * 2 + xl)
        return carry

    lax.fori_loop(1, 64, greet_plane, 0)
    lax.fori_loop(1, 16, greet_exp, 0)
    lax.fori_loop(0, 21, greet_acts, 0)
    lax.fori_loop(0, 21, greet_down, 0)

    data = hidden[...].astype(jnp.float32)
    scale = lax.rsqrt(jnp.mean(data * data, axis=1, keepdims=True) + EPSILON)
    normed = data * scale * gain[...]
    line = lax.broadcasted_iota(jnp.int32, (4, FLAG), 0)
    flags = jnp.zeros((4, FLAG), jnp.int32)
    for r in range(4):
        flags = jnp.where(line == r, route[r], flags)
    flags = flags.astype(jnp.float32)
    for j in range(4):
        staged[4 * j : 4 * j + 4, 0:QUARTER] = normed[:, j * QUARTER : (j + 1) * QUARTER]
        staged[4 * j : 4 * j + 4, QUARTER:] = flags
    rows[e] = staged[...].astype(jnp.bfloat16)

    to = lax.broadcasted_iota(jnp.int32, (256, 256), 0)
    source = lax.broadcasted_iota(jnp.int32, (256, 256), 1)
    wanted = ((to % 64) // 4) * 16 + (to // 64) * 4 + to % 4
    perm[...] = jnp.where(wanted == source, 1.0, 0.0).astype(jnp.bfloat16)

    pl.semaphore_wait(barrier, 63 + 15 + 21 + 21)

    def slot(dy, other):
        return ((y + dy + 8) % 8) * 2 + (1 - xl if other else xl)

    def pass_on(s, ee):
        pltpu.make_async_remote_copy(
            src_ref=rows.at[s], dst_ref=rows.at[s], send_sem=row_send, recv_sem=row_recv.at[s],
            device_id=(g, ee), device_id_type=MESH,
        ).start()

    def row_wait(s):
        pltpu.make_async_copy(rows.at[s], rows.at[s], row_recv.at[s]).wait()

    right, left, across = slot(1, False), slot(-1, False), slot(0, True)
    pass_on(e, across)
    pass_on(e, right)
    pass_on(e, left)

    def a_dest(i):
        k = (xh * 2 + c + i // 8) % 8
        zz = (z + i % 8) % 8
        return k // 2, zz, k % 2

    def a_source(aa, zz, cc):
        column = pl.multiple_of(aa * QUARTER + zz * COLS, 128)
        return sectioned.at[pl.ds(pl.multiple_of(cc * SUB, SUB), SUB), pl.ds(column, COLS)]

    def a_start(i, carry):
        aa, zz, cc = a_dest(i)

        @pl.when(zz < ZW)
        def _():
            pltpu.make_async_remote_copy(
                src_ref=a_source(aa, zz, cc), dst_ref=chunks.at[g], send_sem=a_send, recv_sem=a_recv,
                device_id=(grp(aa, zz, cc), e), device_id_type=MESH,
            ).start()

        return carry

    @pl.when(z < ZW)
    def _():
        pltpu.make_async_copy(a_source(xh, z, c), chunks.at[g], a_local).start()

    lax.fori_loop(1, 64, a_start, 0)

    row_wait(across)
    pass_on(across, right)
    pass_on(across, left)
    for d in (1, 2, 3):
        for other in (False, True):
            s = slot(-d, other)
            row_wait(s)
            if d < 3 or not other:
                pass_on(s, right)
            s = slot(d, other)
            row_wait(s)
            if d < 3 or other:
                pass_on(s, left)
    row_wait(slot(4, False))
    row_wait(slot(4, True))

    load.wait()
    flat = rows[...].reshape(256, QUARTER + FLAG)
    ordered = jnp.dot(perm[...], flat, preferred_element_type=jnp.float32).astype(jnp.bfloat16)
    gates = jnp.zeros((64, 128), jnp.float32)
    ups = jnp.zeros((64, 128), jnp.float32)
    for j in range(4):
        part = ordered[j * 64 : (j + 1) * 64, 0:QUARTER]
        lanes = slice(j * QUARTER, (j + 1) * QUARTER)
        gates += lax.dot_general(
            part, gate_up[0, :, lanes], (((1,), (1,)), ((), ())), preferred_element_type=jnp.float32
        )
        ups += lax.dot_general(
            part, gate_up[1, :, lanes], (((1,), (1,)), ((), ())), preferred_element_type=jnp.float32
        )
    expert = ordered[0:64, QUARTER:].astype(jnp.float32)
    mine = jnp.abs(expert - half.astype(jnp.float32)) < 0.5
    act[...] = jnp.where(mine, jax.nn.silu(gates) * ups, 0.0).astype(jnp.bfloat16)

    def act_place():
        return acts.at[z, :, pl.ds(pl.multiple_of(quarter * 128, 128), 128)]

    def act_start(i, carry):
        zz = (z + i % 8) % 8
        ee = (half * HALF + (quarter + i // 8) % HALF) * 2 + xl

        @pl.when(zz < ZW)
        def _():
            pltpu.make_async_remote_copy(
                src_ref=act, dst_ref=act_place(), send_sem=act_send, recv_sem=act_recv,
                device_id=(grp(xh, zz, c), ee), device_id_type=MESH,
            ).start()

        return carry

    @pl.when(z < ZW)
    def _():
        pltpu.make_async_copy(act, act_place(), act_local).start()

    lax.fori_loop(1, 32, act_start, 0)

    @pl.when(z < ZW)
    def _():
        pltpu.make_async_copy(a_source(xh, z, c), chunks.at[g], a_local).wait()
        wait_for(63, a_recv)
        for b in range(BUCKETS):
            chosen[b] = chunks[owner[b]]

        yy = half * HALF + xh
        place = down.at[quarter, :, c]

        @pl.when(xh == quarter)
        def _():
            pltpu.make_async_copy(chosen, place, w_local).start()

        for i in range(8):
            k = (xh * 2 + c + i) % 8

            def w_start():
                pltpu.make_async_remote_copy(
                    src_ref=chosen, dst_ref=place, send_sem=w_send, recv_sem=w_recv,
                    device_id=(grp(k // 2, z, k % 2), yy * 2 + xl), device_id_type=MESH,
                ).start()

            if i == 0:
                pl.when(xh != quarter)(w_start)
            else:
                w_start()

        pltpu.make_async_copy(act, act_place(), act_local).wait()
        wait_for(62, act_recv)

        @pl.when(xh == quarter)
        def _():
            wait_for(28, w_recv)
            pltpu.make_async_copy(chosen, place, w_local).wait()

        @pl.when(xh != quarter)
        def _():
            wait_for(32, w_recv)

        product[...] = jnp.dot(
            acts[...].reshape(512, 512), down[...].reshape(512, COLS), preferred_element_type=jnp.float32
        )
        for ee in range(16):
            for zz in range(8):
                sends[ee * 32 + zz * 4 : ee * 32 + zz * 4 + 4, :] = product[zz * 64 + ee * 4 : zz * 64 + ee * 4 + 4, :]
        gathered[...] = sends[...].astype(jnp.bfloat16).reshape(16, 32, COLS)

        def y_start(i, carry):
            ee = (e + i) % 16
            pltpu.make_async_remote_copy(
                src_ref=gathered.at[ee], dst_ref=partials.at[e], send_sem=y_send, recv_sem=y_recv,
                device_id=(g, ee), device_id_type=MESH,
            ).start()
            return carry

        lax.fori_loop(1, 16, y_start, 0)
        own = pltpu.make_async_copy(gathered.at[e], partials.at[e], y_local)
        own.start()
        own.wait()
        wait_for(30, y_recv)
        for q in range(4):
            total = jnp.zeros((32, COLS), jnp.float32)
            for hh in range(2):
                for ll in range(2):
                    total += partials[(hh * HALF + q) * 2 + ll].astype(jnp.float32)
            product[q * 32 : q * 32 + 32, :] = total
        for q in range(4):
            for zz in range(8):
                sends[zz * 16 + q * 4 : zz * 16 + q * 4 + 4, :] = product[q * 32 + zz * 4 : q * 32 + zz * 4 + 4, :]
        sums[...] = sends[0:128, :].astype(jnp.bfloat16).reshape(8, 16, COLS)

        for i in range(1, 8):
            zz = (z + i) % 8
            pltpu.make_async_remote_copy(
                src_ref=sums.at[zz], dst_ref=finals.at[z], send_sem=z_send, recv_sem=z_recv,
                device_id=(grp(xh, zz, c), e), device_id_type=MESH,
            ).start()
        own_z = pltpu.make_async_copy(sums.at[z], finals.at[z], z_local)
        own_z.start()
        own_z.wait()

    @pl.when(z < ZW)
    def _():
        wait_for(6, z_recv)

    @pl.when(z == ZW)
    def _():
        wait_for(7, z_recv)

    line = lax.broadcasted_iota(jnp.int32, (4, COLS), 0)
    scaled = jnp.zeros((4, COLS), jnp.float32)
    for r in range(4):
        scaled = jnp.where(line == r, weight[r], scaled)
    sends[0 : ZW * SUB, :] = finals[0:ZW].astype(jnp.float32).reshape(ZW * SUB, COLS)
    for zz in range(ZW):
        for q in range(4):
            lanes = slice(q * QUARTER + zz * COLS, q * QUARTER + (zz + 1) * COLS)
            out[:, lanes] = (sends[zz * 16 + q * 4 : zz * 16 + q * 4 + 4, :] * scaled).astype(jnp.bfloat16)

    pltpu.make_async_copy(rows.at[pl.ds(0, 15)], rows.at[pl.ds(0, 15)], row_send).wait()

    @pl.when(z == ZW)
    def _():
        wait_for(56, a_send)
        wait_for(56, act_send)

    @pl.when(z < ZW)
    def _():
        wait_for(55, a_send)
        wait_for(54, act_send)
        wait_for(30, y_send)
        wait_for(7, z_send)

        @pl.when(xh == quarter)
        def _():
            wait_for(28, w_send)

        @pl.when(xh != quarter)
        def _():
            wait_for(32, w_send)


def per_device(hidden, norm_gain, route, route_weight, resident, sectioned, owner):
    width = hidden.shape[-1]
    vmem, anywhere = pl.BlockSpec(memory_space=pltpu.VMEM), pl.BlockSpec(memory_space=pl.ANY)
    smem = pl.BlockSpec(memory_space=pltpu.SMEM)
    half = lambda *shape: pltpu.VMEM(shape, jnp.bfloat16)
    single = lambda *shape: pltpu.VMEM(shape, jnp.float32)
    dma = pltpu.SemaphoreType.DMA
    result = pl.pallas_call(
        kernel,
        out_shape=jax.ShapeDtypeStruct((4, width), jnp.bfloat16),
        in_specs=[smem, vmem, vmem, smem, smem, anywhere, anywhere],
        out_specs=vmem,
        scratch_shapes=[
            half(2, 128, width),
            single(SUB, QUARTER + FLAG),
            half(16, SUB, QUARTER + FLAG),
            half(256, 256),
            half(64, SUB, COLS),
            half(BUCKETS, SUB, COLS),
            half(4, BUCKETS, 2, SUB, COLS),
            half(64, 128),
            half(8, 64, 512),
            single(512, COLS),
            single(512, COLS),
            half(16, 32, COLS),
            half(8, SUB, COLS),
            half(8, SUB, COLS),
            half(16, 32, COLS),
            dma, dma, dma((16,)), dma, dma, dma, dma, dma, dma, dma, dma, dma, dma, dma, dma, dma, dma, dma,
        ],
        compiler_params=pltpu.CompilerParams(
            collective_id=0, has_side_effects=True, vmem_limit_bytes=60 * 2**20
        ),
    )(
        owner,
        hidden[0],
        norm_gain[None, :],
        route.reshape(4),
        route_weight.reshape(4),
        resident,
        sectioned[0],
    )
    return result[None]


def solution(mesh):
    in_specs = (
        P("grp", "exp", None),
        P(),
        P("grp", "exp", None),
        P("grp", "exp"),
        P(None, "exp", None),
        P("grp", "exp", None),
        P(),
    )
    return jax.shard_map(
        per_device, mesh=mesh, in_specs=in_specs, out_specs=P("grp", "exp", None), check_vma=False
    )
```

```python
import jax
import jax.numpy as jnp
from jax import lax
from jax.experimental import pallas as pl
from jax.experimental.pallas import tpu as pltpu
from jax.sharding import PartitionSpec as P

MESH = pl.DeviceIdType.MESH
BUCKETS = 4
EPSILON = 1e-06
XH, Z, Y = 4, 8, 8
HALF = 4
ZW = 7
SUB = 16
COLS = 256
QUARTER = ZW * COLS
FLAG = 128
SLOTS = 48


def kernel(
    owner, hidden, gain, route, weight, resident, sectioned,
    out,
    gate_up, staged, rows, perm, spread, merge, chunks, chosen, down, act, acts, packed, parts, full,
    partials, sums, finals, gathered,
    local_sem, row_send, row_recv, a_send, a_recv, a_local, w_send, w_recv, w_local, act_send, act_recv, act_local,
    y_send, y_recv, y_local, z_send, z_recv, z_local,
):
    g, e = lax.axis_index("grp"), lax.axis_index("exp")
    xh, z, c = g // 16, (g // 2) % 8, g % 2
    y, xl = e // 2, e % 2
    half, quarter = y // HALF, y % HALF

    def wait_for(blocks, sem):
        pltpu.make_async_copy(chunks.at[pl.ds(0, blocks)], chunks.at[pl.ds(0, blocks)], sem).wait()

    def wait_slots(blocks, sem):
        ref = gate_up.at[0, pl.ds(0, SLOTS), pl.ds(0, blocks * 128)]
        pltpu.make_async_copy(ref, ref, sem).wait()

    def grp(a, b, d):
        return (a * Z + b) * 2 + d

    load = pltpu.make_async_copy(resident, gate_up, local_sem)
    load.start()

    barrier = pltpu.get_barrier_semaphore()

    def greet(gg, ee):
        pl.semaphore_signal(barrier, inc=1, device_id=(gg, ee), device_id_type=MESH)

    def greet_plane(i, carry):
        greet((g + i) % 64, e)
        return carry

    def greet_exp(i, carry):
        greet(g, (e + i) % 16)
        return carry

    def greet_acts(i, carry):
        greet(grp(xh, (z + 1 + i % 7) % Z, c), (half * HALF + (quarter + 1 + i // 7) % HALF) * 2 + xl)
        return carry

    def greet_down(i, carry):
        k = (xh * 2 + c + 1 + i % 7) % 8
        greet(grp(k // 2, z, k % 2), (half * HALF + (quarter + 1 + i // 7) % HALF) * 2 + xl)
        return carry

    lax.fori_loop(1, 64, greet_plane, 0)
    lax.fori_loop(1, 16, greet_exp, 0)
    lax.fori_loop(0, 21, greet_acts, 0)
    lax.fori_loop(0, 21, greet_down, 0)

    data = hidden[...].astype(jnp.float32)
    scale = lax.rsqrt(jnp.mean(data * data, axis=1, keepdims=True) + EPSILON)
    normed = data * scale * gain[...]
    zeros = 4 - (route[0] + route[1] + route[2] + route[3])
    place_of, seen0, seen1 = [], 0, zeros
    for r in range(4):
        place_of.append(jnp.where(route[r] == 0, seen0, seen1))
        seen0, seen1 = seen0 + 1 - route[r], seen1 + route[r]
    line = lax.broadcasted_iota(jnp.int32, normed.shape, 0)
    ranked = jnp.zeros_like(normed)
    for r in range(4):
        ranked = jnp.where(line == place_of[r], jnp.broadcast_to(normed[r : r + 1], normed.shape), ranked)
    normed = ranked
    flags = jnp.where(lax.broadcasted_iota(jnp.int32, (4, FLAG), 0) >= zeros, 1.0, 0.0)
    for j in range(4):
        staged[4 * j : 4 * j + 4, 0:QUARTER] = normed[:, j * QUARTER : (j + 1) * QUARTER]
        staged[4 * j : 4 * j + 4, QUARTER:] = flags
    rows[e] = staged[...].astype(jnp.bfloat16)

    def ones(shape, wanted):
        source = lax.broadcasted_iota(jnp.int32, shape, 1)
        return jnp.where(wanted == source, 1.0, 0.0)

    t = lax.broadcasted_iota(jnp.int32, (4 * SLOTS, 256), 0)
    j4 = jnp.where(t >= SLOTS, 1, 0) + jnp.where(t >= 2 * SLOTS, 1, 0) + jnp.where(t >= 3 * SLOTS, 1, 0)
    u = t - SLOTS * j4
    dev = (u * 43) >> 7
    perm[...] = ones((4 * SLOTS, 256), dev * 16 + j4 * 4 + (u - 3 * dev) + half).astype(jnp.bfloat16)
    t = lax.broadcasted_iota(jnp.int32, (8 * SLOTS, 8 * SLOTS), 0)
    dev = (t * 2731) >> 16
    u = t - 24 * dev
    zz = (u * 43) >> 7
    spread[...] = ones((8 * SLOTS, 8 * SLOTS), zz * SLOTS + dev * 3 + (u - 3 * zz)).astype(jnp.bfloat16)
    t = lax.broadcasted_iota(jnp.int32, (128, 4 * SLOTS), 0)
    k = t % 4
    base = ((t // 4) % 4) * SLOTS + (t // 16) * 3 + k
    first = ones((128, 4 * SLOTS), jnp.where(k < 3, base, -1))
    second = ones((128, 4 * SLOTS), jnp.where(k > 0, base + 23, -1))
    merge[...] = (first + second).astype(jnp.bfloat16)

    pl.semaphore_wait(barrier, 63 + 15 + 21 + 21)

    def slot(dy, other):
        return ((y + dy + 8) % 8) * 2 + (1 - xl if other else xl)

    def pass_on(s, ee):
        pltpu.make_async_remote_copy(
            src_ref=rows.at[s], dst_ref=rows.at[s], send_sem=row_send, recv_sem=row_recv.at[s],
            device_id=(g, ee), device_id_type=MESH,
        ).start()

    def row_wait(s):
        pltpu.make_async_copy(rows.at[s], rows.at[s], row_recv.at[s]).wait()

    right, left, across = slot(1, False), slot(-1, False), slot(0, True)
    pass_on(e, across)
    pass_on(e, right)
    pass_on(e, left)

    def a_dest(i):
        k = (xh * 2 + c + i // 8) % 8
        zz = (z + i % 8) % 8
        return k // 2, zz, k % 2

    def a_source(aa, zz, cc):
        column = pl.multiple_of(aa * QUARTER + zz * COLS, 128)
        return sectioned.at[pl.ds(pl.multiple_of(cc * SUB, SUB), SUB), pl.ds(column, COLS)]

    def a_start(i, carry):
        aa, zz, cc = a_dest(i)

        @pl.when(zz < ZW)
        def _():
            pltpu.make_async_remote_copy(
                src_ref=a_source(aa, zz, cc), dst_ref=chunks.at[g], send_sem=a_send, recv_sem=a_recv,
                device_id=(grp(aa, zz, cc), e), device_id_type=MESH,
            ).start()

        return carry

    @pl.when(z < ZW)
    def _():
        pltpu.make_async_copy(a_source(xh, z, c), chunks.at[g], a_local).start()

    lax.fori_loop(1, 64, a_start, 0)

    row_wait(across)
    pass_on(across, right)
    pass_on(across, left)
    for d in (1, 2, 3):
        for other in (False, True):
            s = slot(-d, other)
            row_wait(s)
            if d < 3 or not other:
                pass_on(s, right)
            s = slot(d, other)
            row_wait(s)
            if d < 3 or other:
                pass_on(s, left)
    row_wait(slot(4, False))
    row_wait(slot(4, True))

    load.wait()
    flat = rows[...].reshape(256, QUARTER + FLAG)
    ordered = jnp.dot(perm[...], flat, preferred_element_type=jnp.float32).astype(jnp.bfloat16)
    gates = jnp.zeros((SLOTS, 128), jnp.float32)
    ups = jnp.zeros((SLOTS, 128), jnp.float32)
    for j in range(4):
        part = ordered[j * SLOTS : (j + 1) * SLOTS, 0:QUARTER]
        lanes = slice(j * QUARTER, (j + 1) * QUARTER)
        gates += lax.dot_general(
            part, gate_up[0, :, lanes], (((1,), (1,)), ((), ())), preferred_element_type=jnp.float32
        )
        ups += lax.dot_general(
            part, gate_up[1, :, lanes], (((1,), (1,)), ((), ())), preferred_element_type=jnp.float32
        )
    expert = ordered[0:SLOTS, QUARTER:].astype(jnp.float32)
    mine = jnp.abs(expert - half.astype(jnp.float32)) < 0.5
    act[...] = jnp.where(mine, jax.nn.silu(gates) * ups, 0.0).astype(jnp.bfloat16)

    def act_place():
        return acts.at[z, :, pl.ds(pl.multiple_of(quarter * 128, 128), 128)]

    def act_start(i, carry):
        zz = (z + i % 8) % 8
        ee = (half * HALF + (quarter + i // 8) % HALF) * 2 + xl

        @pl.when(zz < ZW)
        def _():
            pltpu.make_async_remote_copy(
                src_ref=act, dst_ref=act_place(), send_sem=act_send, recv_sem=act_recv,
                device_id=(grp(xh, zz, c), ee), device_id_type=MESH,
            ).start()

        return carry

    @pl.when(z < ZW)
    def _():
        pltpu.make_async_copy(act, act_place(), act_local).start()

    lax.fori_loop(1, 32, act_start, 0)

    @pl.when(z < ZW)
    def _():
        pltpu.make_async_copy(a_source(xh, z, c), chunks.at[g], a_local).wait()
        wait_for(63, a_recv)
        for b in range(BUCKETS):
            chosen[b] = chunks[owner[b]]

        yy = half * HALF + xh
        place = down.at[quarter, :, c]

        @pl.when(xh == quarter)
        def _():
            pltpu.make_async_copy(chosen, place, w_local).start()

        for i in range(8):
            k = (xh * 2 + c + i) % 8

            def w_start():
                pltpu.make_async_remote_copy(
                    src_ref=chosen, dst_ref=place, send_sem=w_send, recv_sem=w_recv,
                    device_id=(grp(k // 2, z, k % 2), yy * 2 + xl), device_id_type=MESH,
                ).start()

            if i == 0:
                pl.when(xh != quarter)(w_start)
            else:
                w_start()

        pltpu.make_async_copy(act, act_place(), act_local).wait()
        wait_slots(31, act_recv)

        @pl.when(xh == quarter)
        def _():
            wait_for(28, w_recv)
            pltpu.make_async_copy(chosen, place, w_local).wait()

        @pl.when(xh != quarter)
        def _():
            wait_for(32, w_recv)

        product = jnp.dot(
            acts[...].reshape(8 * SLOTS, 512), down[...].reshape(512, COLS), preferred_element_type=jnp.float32
        ).astype(jnp.bfloat16)
        by_dev = jnp.dot(spread[...], product, preferred_element_type=jnp.float32)
        for ee in range(16):
            for k in range(2):
                packed[ee * SLOTS + k * 24 : ee * SLOTS + k * 24 + 24, :] = by_dev[
                    ee * 24 : ee * 24 + 24, k * 128 : (k + 1) * 128
                ]
        gathered[...] = packed[...].astype(jnp.bfloat16).reshape(16, SLOTS, 128)

        def y_start(i, carry):
            ee = (e + i) % 16
            pltpu.make_async_remote_copy(
                src_ref=gathered.at[ee], dst_ref=partials.at[e], send_sem=y_send, recv_sem=y_recv,
                device_id=(g, ee), device_id_type=MESH,
            ).start()
            return carry

        lax.fori_loop(1, 16, y_start, 0)
        own = pltpu.make_async_copy(gathered.at[e], partials.at[e], y_local)
        own.start()
        own.wait()
        wait_slots(15, y_recv)
        for q in range(4):
            for hh in range(2):
                source = (hh * HALF + q) * 2
                total = partials[source].astype(jnp.float32) + partials[source + 1].astype(jnp.float32)
                for k in range(2):
                    parts[q * SLOTS + hh * 24 : q * SLOTS + hh * 24 + 24, k * 128 : (k + 1) * 128] = total[
                        k * 24 : k * 24 + 24
                    ]
        merged = jnp.dot(merge[...], parts[...].astype(jnp.bfloat16), preferred_element_type=jnp.float32)
        sums[...] = merged.astype(jnp.bfloat16).reshape(8, 16, COLS)

        for i in range(1, 8):
            zz = (z + i) % 8
            pltpu.make_async_remote_copy(
                src_ref=sums.at[zz], dst_ref=finals.at[z], send_sem=z_send, recv_sem=z_recv,
                device_id=(grp(xh, zz, c), e), device_id_type=MESH,
            ).start()
        own_z = pltpu.make_async_copy(sums.at[z], finals.at[z], z_local)
        own_z.start()
        own_z.wait()

    @pl.when(z < ZW)
    def _():
        wait_for(6, z_recv)

    @pl.when(z == ZW)
    def _():
        wait_for(7, z_recv)

    parts[0 : ZW * SUB, :] = finals[0:ZW].astype(jnp.float32).reshape(ZW * SUB, COLS)
    for zz in range(ZW):
        for q in range(4):
            lanes = slice(q * QUARTER + zz * COLS, q * QUARTER + (zz + 1) * COLS)
            full[:, lanes] = parts[zz * 16 + q * 4 : zz * 16 + q * 4 + 4, :]
    line = lax.broadcasted_iota(jnp.int32, full.shape, 0)
    result = jnp.zeros(full.shape, jnp.float32)
    for k in range(4):
        share = jnp.zeros(full.shape, jnp.float32)
        for r in range(4):
            share = jnp.where(line == r, jnp.where(place_of[r] == k, weight[r], 0.0), share)
        result += share * full[k : k + 1, :]
    out[...] = result.astype(jnp.bfloat16)

    pltpu.make_async_copy(rows.at[pl.ds(0, 15)], rows.at[pl.ds(0, 15)], row_send).wait()

    @pl.when(z == ZW)
    def _():
        wait_for(56, a_send)
        wait_slots(28, act_send)

    @pl.when(z < ZW)
    def _():
        wait_for(55, a_send)
        wait_slots(27, act_send)
        wait_slots(15, y_send)
        wait_for(7, z_send)

        @pl.when(xh == quarter)
        def _():
            wait_for(28, w_send)

        @pl.when(xh != quarter)
        def _():
            wait_for(32, w_send)


def per_device(hidden, norm_gain, route, route_weight, resident, sectioned, owner):
    width = hidden.shape[-1]
    vmem, anywhere = pl.BlockSpec(memory_space=pltpu.VMEM), pl.BlockSpec(memory_space=pl.ANY)
    smem = pl.BlockSpec(memory_space=pltpu.SMEM)
    half = lambda *shape: pltpu.VMEM(shape, jnp.bfloat16)
    single = lambda *shape: pltpu.VMEM(shape, jnp.float32)
    dma = pltpu.SemaphoreType.DMA
    result = pl.pallas_call(
        kernel,
        out_shape=jax.ShapeDtypeStruct((4, width), jnp.bfloat16),
        in_specs=[smem, vmem, vmem, smem, smem, anywhere, anywhere],
        out_specs=vmem,
        scratch_shapes=[
            half(2, 128, width),
            single(SUB, QUARTER + FLAG),
            half(16, SUB, QUARTER + FLAG),
            half(4 * SLOTS, 256),
            half(8 * SLOTS, 8 * SLOTS),
            half(128, 4 * SLOTS),
            half(64, SUB, COLS),
            half(BUCKETS, SUB, COLS),
            half(4, BUCKETS, 2, SUB, COLS),
            half(SLOTS, 128),
            half(8, SLOTS, 512),
            single(16 * SLOTS, 128),
            single(4 * SLOTS, COLS),
            single(4, width),
            half(16, SLOTS, 128),
            half(8, SUB, COLS),
            half(8, SUB, COLS),
            half(16, SLOTS, 128),
            dma, dma, dma((16,)), dma, dma, dma, dma, dma, dma, dma, dma, dma, dma, dma, dma, dma, dma, dma,
        ],
        compiler_params=pltpu.CompilerParams(
            collective_id=0, has_side_effects=True, vmem_limit_bytes=60 * 2**20
        ),
    )(
        owner,
        hidden[0],
        norm_gain[None, :],
        route.reshape(4),
        route_weight.reshape(4),
        resident,
        sectioned[0],
    )
    return result[None]


def solution(mesh):
    in_specs = (
        P("grp", "exp", None),
        P(),
        P("grp", "exp", None),
        P("grp", "exp"),
        P(None, "exp", None),
        P("grp", "exp", None),
        P(),
    )
    return jax.shard_map(
        per_device, mesh=mesh, in_specs=in_specs, out_specs=P("grp", "exp", None), check_vma=False
    )
```

```python
import jax
import jax.numpy as jnp
from jax import lax
from jax.experimental import pallas as pl
from jax.experimental.pallas import tpu as pltpu
from jax.sharding import PartitionSpec as P

MESH = pl.DeviceIdType.MESH
BUCKETS = 4
EPSILON = 1e-06
XH, Z, Y = 4, 8, 8
HALF = 4
ZW = 7
SUB = 16
COLS = 256
QUARTER = ZW * COLS
FLAG = 128
SLOTS = 48


def kernel(
    owner, hidden, gain, route, weight, resident, sectioned,
    out,
    gate_up, staged, rows, perm, spread, merge, chunks, chosen, down, act, acts, packed, parts,
    partials, sums, finals, gathered,
    local_sem, row_send, row_recv, a_send, a_recv, a_local, w_send, w_recv, w_local, act_send, act_recv, act_local,
    y_send, y_recv, y_local, z_send, z_recv, z_local,
):
    g, e = lax.axis_index("grp"), lax.axis_index("exp")
    xh, z, c = g // 16, (g // 2) % 8, g % 2
    y, xl = e // 2, e % 2
    half, quarter = y // HALF, y % HALF

    def wait_for(blocks, sem):
        pltpu.make_async_copy(chunks.at[pl.ds(0, blocks)], chunks.at[pl.ds(0, blocks)], sem).wait()

    def wait_slots(blocks, sem):
        ref = gate_up.at[0, pl.ds(0, SLOTS), pl.ds(0, blocks * 128)]
        pltpu.make_async_copy(ref, ref, sem).wait()

    def grp(a, b, d):
        return (a * Z + b) * 2 + d

    load = pltpu.make_async_copy(resident, gate_up, local_sem)
    load.start()

    barrier = pltpu.get_barrier_semaphore()

    def greet(gg, ee):
        pl.semaphore_signal(barrier, inc=1, device_id=(gg, ee), device_id_type=MESH)

    def greet_plane(i, carry):
        greet((g + i) % 64, e)
        return carry

    def greet_exp(i, carry):
        greet(g, (e + i) % 16)
        return carry

    def greet_acts(i, carry):
        greet(grp(xh, (z + 1 + i % 7) % Z, c), (half * HALF + (quarter + 1 + i // 7) % HALF) * 2 + xl)
        return carry

    def greet_down(i, carry):
        k = (xh * 2 + c + 1 + i % 7) % 8
        greet(grp(k // 2, z, k % 2), (half * HALF + (quarter + 1 + i // 7) % HALF) * 2 + xl)
        return carry

    lax.fori_loop(1, 64, greet_plane, 0)
    lax.fori_loop(1, 16, greet_exp, 0)
    lax.fori_loop(0, 21, greet_acts, 0)
    lax.fori_loop(0, 21, greet_down, 0)

    data = hidden[...].astype(jnp.float32)
    scale = lax.rsqrt(jnp.mean(data * data, axis=1, keepdims=True) + EPSILON)
    normed = data * scale * gain[...]
    zeros = 4 - (route[0] + route[1] + route[2] + route[3])
    place_of, seen0, seen1 = [], 0, zeros
    for r in range(4):
        place_of.append(jnp.where(route[r] == 0, seen0, seen1))
        seen0, seen1 = seen0 + 1 - route[r], seen1 + route[r]
    line = lax.broadcasted_iota(jnp.int32, normed.shape, 0)
    ranked = jnp.zeros_like(normed)
    for r in range(4):
        ranked = jnp.where(line == place_of[r], jnp.broadcast_to(normed[r : r + 1], normed.shape), ranked)
    normed = ranked
    flags = jnp.where(lax.broadcasted_iota(jnp.int32, (4, FLAG), 0) >= zeros, 1.0, 0.0)
    for j in range(4):
        staged[4 * j : 4 * j + 4, 0:QUARTER] = normed[:, j * QUARTER : (j + 1) * QUARTER]
        staged[4 * j : 4 * j + 4, QUARTER:] = flags
    rows[e] = staged[...].astype(jnp.bfloat16)

    pl.semaphore_wait(barrier, 63 + 15 + 21 + 21)

    def slot(dy, other):
        return ((y + dy + 8) % 8) * 2 + (1 - xl if other else xl)

    def pass_on(s, ee):
        pltpu.make_async_remote_copy(
            src_ref=rows.at[s], dst_ref=rows.at[s], send_sem=row_send, recv_sem=row_recv.at[s],
            device_id=(g, ee), device_id_type=MESH,
        ).start()

    def row_wait(s):
        pltpu.make_async_copy(rows.at[s], rows.at[s], row_recv.at[s]).wait()

    right, left, across = slot(1, False), slot(-1, False), slot(0, True)
    pass_on(e, across)
    pass_on(e, right)
    pass_on(e, left)

    def a_dest(i):
        k = (xh * 2 + c + i // 8) % 8
        zz = (z + i % 8) % 8
        return k // 2, zz, k % 2

    def a_source(aa, zz, cc):
        column = pl.multiple_of(aa * QUARTER + zz * COLS, 128)
        return sectioned.at[pl.ds(pl.multiple_of(cc * SUB, SUB), SUB), pl.ds(column, COLS)]

    def a_start(i, carry):
        aa, zz, cc = a_dest(i)

        @pl.when(zz < ZW)
        def _():
            pltpu.make_async_remote_copy(
                src_ref=a_source(aa, zz, cc), dst_ref=chunks.at[g], send_sem=a_send, recv_sem=a_recv,
                device_id=(grp(aa, zz, cc), e), device_id_type=MESH,
            ).start()

        return carry

    @pl.when(z < ZW)
    def _():
        pltpu.make_async_copy(a_source(xh, z, c), chunks.at[g], a_local).start()

    lax.fori_loop(1, 64, a_start, 0)

    def ones(shape, wanted):
        source = lax.broadcasted_iota(jnp.int32, shape, 1)
        return jnp.where(wanted == source, 1.0, 0.0)

    t = lax.broadcasted_iota(jnp.int32, (4 * SLOTS, 256), 0)
    j4 = jnp.where(t >= SLOTS, 1, 0) + jnp.where(t >= 2 * SLOTS, 1, 0) + jnp.where(t >= 3 * SLOTS, 1, 0)
    u = t - SLOTS * j4
    dev = (u * 43) >> 7
    perm[...] = ones((4 * SLOTS, 256), dev * 16 + j4 * 4 + (u - 3 * dev) + half).astype(jnp.bfloat16)

    row_wait(across)
    pass_on(across, right)
    pass_on(across, left)
    for d in (1, 2, 3):
        for other in (False, True):
            s = slot(-d, other)
            row_wait(s)
            if d < 3 or not other:
                pass_on(s, right)
            s = slot(d, other)
            row_wait(s)
            if d < 3 or other:
                pass_on(s, left)
    row_wait(slot(4, False))
    row_wait(slot(4, True))

    load.wait()
    flat = rows[...].reshape(256, QUARTER + FLAG)
    ordered = jnp.dot(perm[...], flat, preferred_element_type=jnp.float32).astype(jnp.bfloat16)
    gates = jnp.zeros((SLOTS, 128), jnp.float32)
    ups = jnp.zeros((SLOTS, 128), jnp.float32)
    for j in range(4):
        part = ordered[j * SLOTS : (j + 1) * SLOTS, 0:QUARTER]
        lanes = slice(j * QUARTER, (j + 1) * QUARTER)
        gates += lax.dot_general(
            part, gate_up[0, :, lanes], (((1,), (1,)), ((), ())), preferred_element_type=jnp.float32
        )
        ups += lax.dot_general(
            part, gate_up[1, :, lanes], (((1,), (1,)), ((), ())), preferred_element_type=jnp.float32
        )
    expert = ordered[0:SLOTS, QUARTER:].astype(jnp.float32)
    mine = jnp.abs(expert - half.astype(jnp.float32)) < 0.5
    act[...] = jnp.where(mine, jax.nn.silu(gates) * ups, 0.0).astype(jnp.bfloat16)

    def act_place():
        return acts.at[z, :, pl.ds(pl.multiple_of(quarter * 128, 128), 128)]

    def act_start(i, carry):
        zz = (z + i % 8) % 8
        ee = (half * HALF + (quarter + i // 8) % HALF) * 2 + xl

        @pl.when(zz < ZW)
        def _():
            pltpu.make_async_remote_copy(
                src_ref=act, dst_ref=act_place(), send_sem=act_send, recv_sem=act_recv,
                device_id=(grp(xh, zz, c), ee), device_id_type=MESH,
            ).start()

        return carry

    @pl.when(z < ZW)
    def _():
        pltpu.make_async_copy(act, act_place(), act_local).start()

    lax.fori_loop(1, 32, act_start, 0)

    t = lax.broadcasted_iota(jnp.int32, (8 * SLOTS, 8 * SLOTS), 0)
    dev = (t * 2731) >> 16
    u = t - 24 * dev
    zz = (u * 43) >> 7
    spread[...] = ones((8 * SLOTS, 8 * SLOTS), zz * SLOTS + dev * 3 + (u - 3 * zz)).astype(jnp.bfloat16)
    t = lax.broadcasted_iota(jnp.int32, (128, 4 * SLOTS), 0)
    k = t % 4
    base = ((t // 4) % 4) * SLOTS + (t // 16) * 3 + k
    first = ones((128, 4 * SLOTS), jnp.where(k < 3, base, -1))
    second = ones((128, 4 * SLOTS), jnp.where(k > 0, base + 23, -1))
    merge[...] = (first + second).astype(jnp.bfloat16)

    line = lax.broadcasted_iota(jnp.int32, (4, COLS), 0)
    shares = []
    for k in range(4):
        share = jnp.zeros((4, COLS), jnp.float32)
        for r in range(4):
            share = jnp.where(line == r, jnp.where(place_of[r] == k, weight[r], 0.0), share)
        shares.append(share)

    @pl.when(z < ZW)
    def _():
        pltpu.make_async_copy(a_source(xh, z, c), chunks.at[g], a_local).wait()
        wait_for(63, a_recv)
        for b in range(BUCKETS):
            chosen[b] = chunks[owner[b]]

        yy = half * HALF + xh
        place = down.at[quarter, :, c]

        @pl.when(xh == quarter)
        def _():
            pltpu.make_async_copy(chosen, place, w_local).start()

        for i in range(8):
            k = (xh * 2 + c + i) % 8

            def w_start():
                pltpu.make_async_remote_copy(
                    src_ref=chosen, dst_ref=place, send_sem=w_send, recv_sem=w_recv,
                    device_id=(grp(k // 2, z, k % 2), yy * 2 + xl), device_id_type=MESH,
                ).start()

            if i == 0:
                pl.when(xh != quarter)(w_start)
            else:
                w_start()

        pltpu.make_async_copy(act, act_place(), act_local).wait()
        wait_slots(31, act_recv)

        @pl.when(xh == quarter)
        def _():
            wait_for(28, w_recv)
            pltpu.make_async_copy(chosen, place, w_local).wait()

        @pl.when(xh != quarter)
        def _():
            wait_for(32, w_recv)

        product = jnp.dot(
            acts[...].reshape(8 * SLOTS, 512), down[...].reshape(512, COLS), preferred_element_type=jnp.float32
        ).astype(jnp.bfloat16)
        by_dev = jnp.dot(spread[...], product, preferred_element_type=jnp.float32)
        for ee in range(16):
            for k in range(2):
                packed[ee * SLOTS + k * 24 : ee * SLOTS + k * 24 + 24, :] = by_dev[
                    ee * 24 : ee * 24 + 24, k * 128 : (k + 1) * 128
                ]
        gathered[...] = packed[...].astype(jnp.bfloat16).reshape(16, SLOTS, 128)

        def y_start(i, carry):
            ee = (e + i) % 16
            pltpu.make_async_remote_copy(
                src_ref=gathered.at[ee], dst_ref=partials.at[e], send_sem=y_send, recv_sem=y_recv,
                device_id=(g, ee), device_id_type=MESH,
            ).start()
            return carry

        lax.fori_loop(1, 16, y_start, 0)
        own = pltpu.make_async_copy(gathered.at[e], partials.at[e], y_local)
        own.start()
        own.wait()
        wait_slots(15, y_recv)
        for q in range(4):
            for hh in range(2):
                source = (hh * HALF + q) * 2
                total = partials[source].astype(jnp.float32) + partials[source + 1].astype(jnp.float32)
                for k in range(2):
                    parts[q * SLOTS + hh * 24 : q * SLOTS + hh * 24 + 24, k * 128 : (k + 1) * 128] = total[
                        k * 24 : k * 24 + 24
                    ]
        merged = jnp.dot(merge[...], parts[...].astype(jnp.bfloat16), preferred_element_type=jnp.float32)
        sums[...] = merged.astype(jnp.bfloat16).reshape(8, 16, COLS)

        for i in range(1, 8):
            zz = (z + i) % 8
            pltpu.make_async_remote_copy(
                src_ref=sums.at[zz], dst_ref=finals.at[z], send_sem=z_send, recv_sem=z_recv,
                device_id=(grp(xh, zz, c), e), device_id_type=MESH,
            ).start()
        own_z = pltpu.make_async_copy(sums.at[z], finals.at[z], z_local)
        own_z.start()
        own_z.wait()

    @pl.when(z < ZW)
    def _():
        wait_for(6, z_recv)

    @pl.when(z == ZW)
    def _():
        wait_for(7, z_recv)

    parts[0 : ZW * SUB, :] = finals[0:ZW].astype(jnp.float32).reshape(ZW * SUB, COLS)
    for zz in range(ZW):
        for q in range(4):
            lanes = slice(q * QUARTER + zz * COLS, q * QUARTER + (zz + 1) * COLS)
            block = parts[zz * 16 + q * 4 : zz * 16 + q * 4 + 4, :]
            total = shares[0] * block[0:1]
            for k in range(1, 4):
                total += shares[k] * block[k : k + 1]
            out[:, lanes] = total.astype(jnp.bfloat16)

    pltpu.make_async_copy(rows.at[pl.ds(0, 15)], rows.at[pl.ds(0, 15)], row_send).wait()

    @pl.when(z == ZW)
    def _():
        wait_for(56, a_send)
        wait_slots(28, act_send)

    @pl.when(z < ZW)
    def _():
        wait_for(55, a_send)
        wait_slots(27, act_send)
        wait_slots(15, y_send)
        wait_for(7, z_send)

        @pl.when(xh == quarter)
        def _():
            wait_for(28, w_send)

        @pl.when(xh != quarter)
        def _():
            wait_for(32, w_send)


def per_device(hidden, norm_gain, route, route_weight, resident, sectioned, owner):
    width = hidden.shape[-1]
    vmem, anywhere = pl.BlockSpec(memory_space=pltpu.VMEM), pl.BlockSpec(memory_space=pl.ANY)
    smem = pl.BlockSpec(memory_space=pltpu.SMEM)
    half = lambda *shape: pltpu.VMEM(shape, jnp.bfloat16)
    single = lambda *shape: pltpu.VMEM(shape, jnp.float32)
    dma = pltpu.SemaphoreType.DMA
    result = pl.pallas_call(
        kernel,
        out_shape=jax.ShapeDtypeStruct((4, width), jnp.bfloat16),
        in_specs=[smem, vmem, vmem, smem, smem, anywhere, anywhere],
        out_specs=vmem,
        scratch_shapes=[
            half(2, 128, width),
            single(SUB, QUARTER + FLAG),
            half(16, SUB, QUARTER + FLAG),
            half(4 * SLOTS, 256),
            half(8 * SLOTS, 8 * SLOTS),
            half(128, 4 * SLOTS),
            half(64, SUB, COLS),
            half(BUCKETS, SUB, COLS),
            half(4, BUCKETS, 2, SUB, COLS),
            half(SLOTS, 128),
            half(8, SLOTS, 512),
            single(16 * SLOTS, 128),
            single(4 * SLOTS, COLS),
            half(16, SLOTS, 128),
            half(8, SUB, COLS),
            half(8, SUB, COLS),
            half(16, SLOTS, 128),
            dma, dma, dma((16,)), dma, dma, dma, dma, dma, dma, dma, dma, dma, dma, dma, dma, dma, dma, dma,
        ],
        compiler_params=pltpu.CompilerParams(
            collective_id=0, has_side_effects=True, vmem_limit_bytes=60 * 2**20
        ),
    )(
        owner,
        hidden[0],
        norm_gain[None, :],
        route.reshape(4),
        route_weight.reshape(4),
        resident,
        sectioned[0],
    )
    return result[None]


def solution(mesh):
    in_specs = (
        P("grp", "exp", None),
        P(),
        P("grp", "exp", None),
        P("grp", "exp"),
        P(None, "exp", None),
        P("grp", "exp", None),
        P(),
    )
    return jax.shard_map(
        per_device, mesh=mesh, in_specs=in_specs, out_specs=P("grp", "exp", None), check_vma=False
    )
```
